32 devices in a mesh: row: 4 (over z), col: 8 (over y, x, core).
Axes of the slice: x: 2, y: 2, z: 4, core: 2. Of those that a mesh axis runs over, the one named last changes fastest.
Arguments:
- updates: float32 [16384, 8192], P('col', 'row'), may hold values from -6 to 6
- block_map: int32 [2, 64], replicated, may hold values from 0 to 79, as said below
- own_diag: float32 [10240], P('row'), may hold values from 2 to 6
- panel_inverse: float32 [512, 512], replicated, as said below
Outputs:
- factor_panel: float32 [10240, 512], P('row')
- trailing: float32 [10240, 10240], P('row', 'col')
The draws below stay inside these ranges and needn't reach their ends.
Inputs may be any that keep to these rules, and one draw needn't show every extreme that they name: `block_map`: within one child the 64 entries name distinct front blocks. Take the child blocks (a, b) held by one device in updates, and the front blocks held by one device in trailing: either exactly 8 of the former land in the latter, or none do. `panel_inverse`: lower triangular with a positive diagonal.
All inputs are finite; a program needn't handle non-finite values.
Results may differ from the reference program's by a relative error of at most 0.000075.
Values sent between devices are 32-bit elements; how exact they have to be, the bound alone decides.
A program may use at most 128 MiB of HBM per device.

```python
import math
import jax
import jax.numpy as jnp
from jax import lax

F = 10240
M = 8192
BLK = 128
PANEL = 512
MB = 64
N_ROW = 4
N_COL = 8


def draw_block_map(key, part):
    front_blocks = F // BLK
    col_blocks = front_blocks // N_COL
    per_col = MB // N_COL
    ratio = N_COL // N_ROW

    def child_draw(child_key):
        row_key, sub_key, slot_base = jax.random.split(child_key, 3)
        row_order = jax.random.permutation(row_key, N_ROW)
        sub_order = jax.random.permutation(sub_key, ratio)
        residue = jnp.arange(N_COL, dtype=jnp.int32)
        col_owner_of = row_order[residue % N_ROW] * ratio + sub_order[residue // N_ROW]
        slot_keys = jax.random.split(slot_base, N_COL)
        offsets = jax.vmap(lambda slot_key: jax.random.permutation(slot_key, col_blocks)[:per_col])(slot_keys)
        child_block = jnp.arange(MB, dtype=jnp.int32)
        owner_col = col_owner_of[child_block % N_COL]
        within = offsets[owner_col, child_block // N_COL]
        return (owner_col * col_blocks + within).astype(jnp.int32)
    return jnp.stack([child_draw(jax.random.fold_in(key, 11)), child_draw(jax.random.fold_in(key, 23))])


def draw_panel_inverse(key, part):
    lower_key, diag_key = jax.random.split(key)
    lower_part = jax.random.normal(lower_key, (PANEL, PANEL), jnp.float32)
    diag_part = jax.random.uniform(diag_key, (PANEL,), jnp.float32, 0.1, 0.3)
    row_ids = jnp.arange(PANEL)[:, None]
    col_ids = jnp.arange(PANEL)[None, :]
    strict_part = jnp.where(row_ids > col_ids, lower_part * (0.15 / math.sqrt(PANEL)), 0.0)
    return (strict_part + jnp.where(row_ids == col_ids, diag_part[None, :], 0.0)).astype(jnp.float32)


def level_of(key, dims, cuts, low, top_value):
    def one(axis_at, blocks):
        draws = jax.random.uniform(jax.random.fold_in(jax.random.fold_in(key, 6), axis_at), (blocks,), jnp.float32, low / len(cuts), top_value / len(cuts))
        return jnp.repeat(jnp.exp(draws), dims[axis_at] // blocks).reshape((-1,) + (1,) * (len(dims) - axis_at - 1))

    loudness = one(*cuts[0])
    for cut in cuts[1:]:
        loudness = loudness * one(*cut)
    return loudness


def centred(key, shape, spread, reach, pieces=(), kind=jnp.bfloat16):
    array = spread * jax.random.normal(key, shape, jnp.float32)
    if pieces:
        array = array * level_of(key, shape, pieces, -0.22, 0.18)
    return jnp.clip(array, -reach, reach).astype(kind)


def setup_inputs(seed: int = 0) -> dict:
    keys = jax.random.split(jax.random.key(seed), 5)
    return {
        "updates": centred(keys[0], (2 * M, M), 1.0, 6.0, ((0, 8), (1, 4)), jnp.float32),
        "block_map": draw_block_map(jax.random.fold_in(keys[4], 71), 0),
        "own_diag": jnp.clip(2.0 + 4.0 * jax.random.uniform(keys[2], (F,), jnp.float32) ** level_of(keys[2], (F,), ((0, 4),), -0.2, 0.2), 2.0, 6.0),
        "panel_inverse": draw_panel_inverse(jax.random.fold_in(keys[4], 71), 0),
    }


def reference(updates, block_map, own_diag, panel_inverse):
    blocks = F // BLK
    front_full = jnp.zeros((blocks, blocks, BLK, BLK), jnp.float32)
    for child_id in range(2):
        child_tiles = updates[child_id * M:(child_id + 1) * M].reshape(MB, BLK, MB, BLK).transpose(0, 2, 1, 3)
        mapping = block_map[child_id].astype(jnp.int32)
        front_full = front_full.at[mapping[:, None], mapping[None, :]].add(child_tiles)
    front_full = front_full.transpose(0, 2, 1, 3).reshape(F, F) + jnp.diag(own_diag)
    factor_panel = jnp.dot(front_full[:, :PANEL], panel_inverse.T, precision=lax.Precision.HIGHEST, preferred_element_type=jnp.float32)
    trailing = front_full - jnp.dot(factor_panel, factor_panel.T, precision=lax.Precision.HIGHEST, preferred_element_type=jnp.float32)
    return factor_panel, trailing
```

```python
import functools
import jax
import jax.numpy as jnp
from jax import lax
from jax.experimental import pallas as pl
from jax.experimental.pallas import tpu as pltpu
from jax.sharding import PartitionSpec as P

BLK = 128
STEP = 256
MIB = 1 << 20


def pick(flags, values):
    return jnp.sum(jnp.where(flags, values, 0), axis=-1, dtype=jnp.int32)


def split(x):
    high = x.astype(jnp.bfloat16)
    low = (x - high.astype(jnp.float32)).astype(jnp.bfloat16)
    return high, low


def dot3(ah, al, bh, bl):
    d = functools.partial(
        lax.dot_general,
        dimension_numbers=(((1,), (1,)), ((), ())),
        preferred_element_type=jnp.float32,
    )
    return d(ah, bh) + (d(ah, bl) + d(al, bh))


def ranks(owner):
    n = owner.shape[-1]
    earlier = jnp.arange(n)[:, None] > jnp.arange(n)[None, :]
    same = owner[..., :, None] == owner[..., None, :]
    return jnp.sum((same & earlier).astype(jnp.int32), axis=-1)


def selection(owner, count, each):
    rank = ranks(owner)
    wanted = (owner[None, None, :] == jnp.arange(count)[:, None, None]) & (
        rank[None, None, :] == jnp.arange(each)[None, :, None]
    )
    return pick(wanted, jnp.arange(owner.shape[0], dtype=jnp.int32))


def pack_kernel(rows_ref, cols_ref, x_ref, o_ref, *, col_count, per_col):
    for t in range(col_count):
        for w in range(per_col):
            j = cols_ref[t * per_col + w]
            o_ref[0, t, 0, w] = x_ref[:, pl.ds(pl.multiple_of(j * BLK, BLK), BLK)]


def pack(updates, rowsel, colsel, row_count, col_count, per_row, per_col):
    width = updates.shape[1]
    grid = pltpu.PrefetchScalarGridSpec(
        num_scalar_prefetch=2,
        grid=(row_count * per_row,),
        in_specs=[pl.BlockSpec((BLK, width), lambda g, r, c: (r[g], 0))],
        out_specs=pl.BlockSpec(
            (1, col_count, 1, per_col, BLK, BLK),
            lambda g, r, c: (g // per_row, 0, g % per_row, 0, 0, 0),
        ),
    )
    return pl.pallas_call(
        functools.partial(pack_kernel, col_count=col_count, per_col=per_col),
        grid_spec=grid,
        out_shape=jax.ShapeDtypeStruct(
            (row_count, col_count, per_row, per_col, BLK, BLK), jnp.float32
        ),
        compiler_params=pltpu.CompilerParams(vmem_limit_bytes=32 * MIB),
    )(rowsel.reshape(-1), colsel.reshape(-1), updates)


def block_sum(recv_ref, rtab, ctab, x, y, front_rows, front_cols):
    total = None
    for c in range(2):
        r = rtab[c * front_rows + x]
        k = ctab[c * front_cols + y]
        good = (r >= 0) & (k >= 0)
        tile = recv_ref[jnp.where(good, r + k, 0)]
        tile = jnp.where(good, tile, 0.0)
        total = tile if total is None else total + tile
    return total


def eye_mask():
    i = lax.broadcasted_iota(jnp.int32, (BLK, BLK), 0)
    j = lax.broadcasted_iota(jnp.int32, (BLK, BLK), 1)
    return i == j


def finish_kernel(rtab, ctab, dtab, recv_ref, diag_ref, factor_ref, across_ref, o_ref, ah, al,
                  *, front_rows, front_cols, chunk):
    g = pl.program_id(0)

    @pl.when(g == 0)
    def _():
        h, l = split(across_ref[...])
        ah[...] = h
        al[...] = l

    fh, fl = split(factor_ref[...])
    eye = eye_mask()
    for base in range(0, front_cols, chunk):
        rows = pl.ds(base * BLK, chunk * BLK)
        term = dot3(fh, fl, ah[rows, :], al[rows, :])
        for p in range(STEP // BLK):
            x = g * (STEP // BLK) + p
            drow = diag_ref[pl.ds(x, 1), :]
            for y in range(base, base + chunk):
                tile = block_sum(recv_ref, rtab, ctab, x, y, front_rows, front_cols)
                on = eye & (dtab[0] + x == dtab[1] + y)
                tile = tile + jnp.where(on, drow, 0.0)
                o_ref[p * BLK:(p + 1) * BLK, y * BLK:(y + 1) * BLK] = (
                    tile - term[p * BLK:(p + 1) * BLK, (y - base) * BLK:(y - base + 1) * BLK]
                )


def finish(rtab, ctab, dtab, recv, diag, factor, across):
    height, panel = factor.shape
    width = across.shape[0]
    front_rows, front_cols = height // BLK, width // BLK
    chunk = 5 if front_cols % 5 == 0 else 1
    once = dict(pipeline_mode=pl.Buffered(1))
    grid = pltpu.PrefetchScalarGridSpec(
        num_scalar_prefetch=3,
        grid=(height // STEP,),
        in_specs=[
            pl.BlockSpec(recv.shape, lambda g, *_: (0, 0, 0), **once),
            pl.BlockSpec(diag.shape, lambda g, *_: (0, 0), **once),
            pl.BlockSpec((STEP, panel), lambda g, *_: (g, 0)),
            pl.BlockSpec((width, panel), lambda g, *_: (0, 0), **once),
        ],
        out_specs=pl.BlockSpec((STEP, width), lambda g, *_: (g, 0)),
        scratch_shapes=[pltpu.VMEM((width, panel), jnp.bfloat16)] * 2,
    )
    return pl.pallas_call(
        functools.partial(finish_kernel, front_rows=front_rows, front_cols=front_cols, chunk=chunk),
        grid_spec=grid,
        out_shape=jax.ShapeDtypeStruct((height, width), jnp.float32),
        compiler_params=pltpu.CompilerParams(vmem_limit_bytes=48 * MIB),
    )(rtab, ctab, dtab, recv, diag, factor, across)


def raw_kernel(rtab, ctab, dtab, recv_ref, diag_ref, o_ref, *, front_rows, front_cols, panel_cols):
    eye = eye_mask()

    @pl.loop(0, front_rows)
    def _(x):
        drow = diag_ref[pl.ds(x, 1), :]
        for y in range(panel_cols):
            tile = block_sum(recv_ref, rtab, ctab, x, y, front_rows, front_cols)
            tile = tile + jnp.where(eye & (dtab[0] + x == dtab[1] + y), drow, 0.0)
            o_ref[pl.ds(pl.multiple_of(x * BLK, BLK), BLK), y * BLK:(y + 1) * BLK] = tile


def raw_panel_of(rtab, ctab, dtab, recv, diag, front_rows, front_cols, panel):
    smem = pl.BlockSpec(memory_space=pltpu.SMEM)
    vmem = pl.BlockSpec(memory_space=pltpu.VMEM)
    return pl.pallas_call(
        functools.partial(raw_kernel, front_rows=front_rows, front_cols=front_cols,
                          panel_cols=panel // BLK),
        in_specs=[smem, smem, smem, vmem, vmem],
        out_specs=vmem,
        out_shape=jax.ShapeDtypeStruct((front_rows * BLK, panel), jnp.float32),
        compiler_params=pltpu.CompilerParams(vmem_limit_bytes=40 * MIB),
    )(rtab, ctab, dtab, recv, diag)


def tables(block_map, row_count, col_count, row_items, col_items, front_rows, front_cols,
           per_row, per_col, my_row, my_col):
    half = col_count // 2
    child_blocks = block_map.shape[1]
    cap = per_row * per_col
    child = jnp.where(my_col >= half, block_map[1], block_map[0])
    row_parent = pick(
        (my_col % half * row_items + jnp.arange(row_items))[:, None] == jnp.arange(child_blocks)[None, :],
        child[None, :],
    )
    col_parent = pick(
        (my_row * col_items + jnp.arange(col_items))[:, None] == jnp.arange(child_blocks)[None, :],
        child[None, :],
    )
    rowsel = selection(row_parent // front_rows, row_count, per_row)
    colsel = selection(col_parent // front_cols, col_count, per_col)
    ids = jnp.arange(child_blocks, dtype=jnp.int32)
    row_rank = ranks((block_map // front_rows).reshape(2, -1, row_items)).reshape(2, -1)
    col_rank = ranks((block_map // front_cols).reshape(2, -1, col_items)).reshape(2, -1)
    source_col = jnp.arange(2, dtype=jnp.int32)[:, None] * half + ids[None, :] // row_items
    row_value = source_col * cap + row_rank * per_col
    col_value = (ids[None, :] // col_items) * (col_count * cap) + col_rank
    at_row = block_map[:, None, :] == (my_row * front_rows + jnp.arange(front_rows))[None, :, None]
    at_col = block_map[:, None, :] == (my_col * front_cols + jnp.arange(front_cols))[None, :, None]
    rtab = pick(at_row, row_value[:, None, :] + 1) - 1
    ctab = pick(at_col, col_value[:, None, :] + 1) - 1
    return rowsel, colsel, rtab.reshape(-1), ctab.reshape(-1)


def on_device(updates, block_map, own_diag, panel_inverse):
    row_count, col_count = lax.axis_size("row"), lax.axis_size("col")
    my_row, my_col = lax.axis_index("row"), lax.axis_index("col")
    devices = row_count * col_count
    row_items, col_items = updates.shape[0] // BLK, updates.shape[1] // BLK
    per_row, per_col = max(1, row_items // row_count), max(1, col_items // col_count)
    height = own_diag.shape[0]
    width = height * row_count // col_count
    panel = panel_inverse.shape[0]
    front_rows, front_cols = height // BLK, width // BLK
    rowsel, colsel, rtab, ctab = tables(
        block_map, row_count, col_count, row_items, col_items, front_rows, front_cols,
        per_row, per_col, my_row, my_col,
    )
    dtab = jnp.stack([my_row * front_rows, my_col * front_cols]).astype(jnp.int32)
    diag = own_diag.reshape(front_rows, BLK)
    outgoing = pack(updates, rowsel, colsel, row_count, col_count, per_row, per_col)
    incoming = lax.all_to_all(
        outgoing.reshape(devices, per_row * per_col, BLK, BLK),
        ("row", "col"), split_axis=0, concat_axis=0, tiled=True,
    ).reshape(-1, BLK, BLK)
    raw = raw_panel_of(rtab, ctab, dtab, incoming, diag, front_rows, front_cols, panel)
    raw = lax.psum(jnp.where(my_col == 0, raw, 0.0), "col")
    factor = lax.dot_general(
        raw, panel_inverse, (((1,), (1,)), ((), ())),
        precision=lax.Precision.HIGHEST, preferred_element_type=jnp.float32,
    )
    start = my_col * width
    mine = start // height == my_row
    across = lax.dynamic_slice_in_dim(factor, start % height, width, 0)
    across = lax.psum(jnp.where(mine, across, 0.0), "row")
    trailing = finish(rtab, ctab, dtab, incoming, diag, factor, across)
    return (factor, trailing)


def solution(mesh):
    return jax.shard_map(
        on_device,
        mesh=mesh,
        in_specs=(P("col", "row"), P(), P("row"), P()),
        out_specs=(P("row", None), P("row", "col")),
        check_vma=False,
    )
```

```python
import functools
import jax
import jax.numpy as jnp
from jax import lax
from jax.experimental import pallas as pl
from jax.experimental.pallas import tpu as pltpu
from jax.sharding import PartitionSpec as P

BLK = 128
STEP = 256
MIB = 1 << 20


def pick(flags, values):
    return jnp.sum(jnp.where(flags, values, 0), axis=-1, dtype=jnp.int32)


def split(x):
    high = x.astype(jnp.bfloat16)
    low = (x - high.astype(jnp.float32)).astype(jnp.bfloat16)
    return high, low


def dot3(ah, al, bh, bl):
    d = functools.partial(
        lax.dot_general,
        dimension_numbers=(((1,), (1,)), ((), ())),
        preferred_element_type=jnp.float32,
    )
    return d(ah, bh) + (d(ah, bl) + d(al, bh))


def ranks(owner):
    n = owner.shape[-1]
    earlier = jnp.arange(n)[:, None] > jnp.arange(n)[None, :]
    same = owner[..., :, None] == owner[..., None, :]
    return jnp.sum((same & earlier).astype(jnp.int32), axis=-1)


def selection(owner, count, each):
    rank = ranks(owner)
    wanted = (owner[None, None, :] == jnp.arange(count)[:, None, None]) & (
        rank[None, None, :] == jnp.arange(each)[None, :, None]
    )
    return pick(wanted, jnp.arange(owner.shape[0], dtype=jnp.int32))


def pack_kernel(rows_ref, cols_ref, x_ref, o_ref, *, col_count, per_col):
    for t in range(col_count):
        for w in range(per_col):
            j = cols_ref[t * per_col + w]
            o_ref[0, t, 0, w] = x_ref[:, pl.ds(pl.multiple_of(j * BLK, BLK), BLK)]


def pack(updates, rowsel, colsel, row_count, col_count, per_row, per_col):
    width = updates.shape[1]
    grid = pltpu.PrefetchScalarGridSpec(
        num_scalar_prefetch=2,
        grid=(row_count * per_row,),
        in_specs=[pl.BlockSpec((BLK, width), lambda g, r, c: (r[g], 0))],
        out_specs=pl.BlockSpec(
            (1, col_count, 1, per_col, BLK, BLK),
            lambda g, r, c: (g // per_row, 0, g % per_row, 0, 0, 0),
        ),
    )
    return pl.pallas_call(
        functools.partial(pack_kernel, col_count=col_count, per_col=per_col),
        grid_spec=grid,
        out_shape=jax.ShapeDtypeStruct(
            (row_count, col_count, per_row, per_col, BLK, BLK), jnp.float32
        ),
        compiler_params=pltpu.CompilerParams(vmem_limit_bytes=32 * MIB),
    )(rowsel.reshape(-1), colsel.reshape(-1), updates)


def block_sum(recv_ref, rtab, ctab, x, y, front_rows, front_cols):
    total = None
    for c in range(2):
        r = rtab[c * front_rows + x]
        k = ctab[c * front_cols + y]
        good = (r >= 0) & (k >= 0)
        tile = recv_ref[jnp.where(good, r + k, 0)]
        tile = jnp.where(good, tile, 0.0)
        total = tile if total is None else total + tile
    return total


def eye_mask():
    i = lax.broadcasted_iota(jnp.int32, (BLK, BLK), 0)
    j = lax.broadcasted_iota(jnp.int32, (BLK, BLK), 1)
    return i == j


def finish_kernel(rtab, ctab, dtab, recv_ref, diag_ref, factor_ref, across_ref, copy_ref, o_ref, ah, al,
                  *, front_rows, front_cols, chunk):
    g = pl.program_id(0)

    @pl.when(g == 0)
    def _():
        h, l = split(across_ref[...])
        ah[...] = h
        al[...] = l

    f = factor_ref[...]
    copy_ref[...] = f
    fh, fl = split(f)
    eye = eye_mask()
    for base in range(0, front_cols, chunk):
        rows = pl.ds(base * BLK, chunk * BLK)
        term = dot3(fh, fl, ah[rows, :], al[rows, :])
        for p in range(STEP // BLK):
            x = g * (STEP // BLK) + p
            drow = diag_ref[pl.ds(x, 1), :]
            for y in range(base, base + chunk):
                tile = block_sum(recv_ref, rtab, ctab, x, y, front_rows, front_cols)
                on = eye & (dtab[0] + x == dtab[1] + y)
                tile = tile + jnp.where(on, drow, 0.0)
                o_ref[p * BLK:(p + 1) * BLK, y * BLK:(y + 1) * BLK] = (
                    tile - term[p * BLK:(p + 1) * BLK, (y - base) * BLK:(y - base + 1) * BLK]
                )


def finish(rtab, ctab, dtab, recv, diag, factor, across):
    height, panel = factor.shape
    width = across.shape[0]
    front_rows, front_cols = height // BLK, width // BLK
    chunk = 5 if front_cols % 5 == 0 else 1
    once = dict(pipeline_mode=pl.Buffered(1))
    grid = pltpu.PrefetchScalarGridSpec(
        num_scalar_prefetch=3,
        grid=(height // STEP,),
        in_specs=[
            pl.BlockSpec(recv.shape, lambda g, *_: (0, 0, 0), **once),
            pl.BlockSpec(diag.shape, lambda g, *_: (0, 0), **once),
            pl.BlockSpec((STEP, panel), lambda g, *_: (g, 0)),
            pl.BlockSpec((width, panel), lambda g, *_: (0, 0), **once),
        ],
        out_specs=[
            pl.BlockSpec((STEP, panel), lambda g, *_: (g, 0)),
            pl.BlockSpec((STEP, width), lambda g, *_: (g, 0)),
        ],
        scratch_shapes=[pltpu.VMEM((width, panel), jnp.bfloat16)] * 2,
    )
    return pl.pallas_call(
        functools.partial(finish_kernel, front_rows=front_rows, front_cols=front_cols, chunk=chunk),
        grid_spec=grid,
        out_shape=[
            jax.ShapeDtypeStruct((height, panel), jnp.float32),
            jax.ShapeDtypeStruct((height, width), jnp.float32),
        ],
        compiler_params=pltpu.CompilerParams(vmem_limit_bytes=48 * MIB),
    )(rtab, ctab, dtab, recv, diag, factor, across)


def exchange_kernel(rtab, ctab, send_ref, diag_ref, inv_ref, recv_ref, factor_ref, across_ref,
                    stage, raw, fact, chunks, inv_high, inv_low,
                    out_sem, in_sem, self_sem, stage_sem, scatter_send, scatter_recv,
                    z_send, z_recv, row_send, row_recv, a_send, a_recv, local_sem, a_local,
                    *, rows_n, cols_n, front_rows, front_cols, panel_cols):
    r, c = lax.axis_index("row"), lax.axis_index("col")
    total = rows_n * cols_n
    me = r * cols_n + c
    half = cols_n // 2
    ratio = cols_n // rows_n
    per_width = cols_n // ratio
    size = chunks.shape[1]
    mesh_id = pl.DeviceIdType.MESH

    def each(count, body):
        def step(n, carry):
            body(n)
            return carry
        lax.fori_loop(0, count, step, 0)

    def at(k):
        return pl.ds(pl.multiple_of(k * size, 8), size)

    barrier = pltpu.get_barrier_semaphore()

    def greet(n):
        t = lax.rem(me + n + 1, total)
        pl.semaphore_signal(barrier, inc=1, device_id=(t // cols_n, lax.rem(t, cols_n)),
                            device_id_type=mesh_id)
    each(total - 1, greet)
    pl.semaphore_wait(barrier, total - 1)

    def tiles(t_row, t_col, source, t):
        return pltpu.make_async_remote_copy(
            src_ref=send_ref.at[t], dst_ref=recv_ref.at[source],
            send_sem=out_sem.at[t], recv_sem=in_sem.at[source],
            device_id=(t_row, t_col), device_id_type=mesh_id)

    def send(n):
        g, i = n // half, lax.rem(n, half)
        t_col = 2 * lax.rem(i + c // 2, half) + g // rows_n
        t_row = lax.rem(r + g + i, rows_n)
        t = t_row * cols_n + t_col

        @pl.when(t != me)
        def _():
            tiles(t_row, t_col, me, t).start()
    each(total, send)
    own = pltpu.make_async_copy(send_ref.at[me], recv_ref.at[me], self_sem)
    own.start()

    def wait_tiles():
        def one(n):
            t = lax.rem(me + n + 1, total)
            tiles(t // cols_n, lax.rem(t, cols_n), t, t).wait_recv()
        each(total - 1, one)
        own.wait()

    def scatter(k):
        return pltpu.make_async_remote_copy(
            src_ref=fact.at[at(k), :], dst_ref=chunks.at[r],
            send_sem=scatter_send.at[k], recv_sem=scatter_recv,
            device_id=(r, k), device_id_type=mesh_id)

    whole = pltpu.make_async_copy(fact, factor_ref, local_sem)

    @pl.when(c == 0)
    def _():
        wait_tiles()
        load = pltpu.make_async_copy(recv_ref, stage, stage_sem)
        load.start()
        h, l = split(inv_ref[...])
        inv_high[...] = h
        inv_low[...] = l
        load.wait()
        eye = eye_mask()
        cap = stage.shape[1]

        def assemble(x):
            drow = diag_ref[pl.ds(x, 1), :]
            for y in range(panel_cols):
                tile = jnp.where(eye & (r * front_rows + x == y), drow, 0.0)
                for child in range(2):
                    a = rtab[child * front_rows + x]
                    b = ctab[child * front_cols + y]
                    good = (a >= 0) & (b >= 0)
                    slot = jnp.where(good, a + b, 0)
                    tile = tile + jnp.where(good, stage[slot // cap, lax.rem(slot, cap)], 0.0)
                raw[pl.ds(pl.multiple_of(x * BLK, BLK), BLK), y * BLK:(y + 1) * BLK] = tile
        each(front_rows, assemble)

        def multiply(n):
            k = cols_n - 1 - n
            h, l = split(raw[at(k), :])
            fact[at(k), :] = dot3(h, l, inv_high[...], inv_low[...])

            @pl.when(k != 0)
            def _():
                scatter(k).start()
        each(cols_n, multiply)
        chunks[r] = fact[0:size, :]
        whole.start()

    @pl.when(c != 0)
    def _():
        scatter(c).wait_recv()

    def along_z(peer, slot):
        return pltpu.make_async_remote_copy(
            src_ref=chunks.at[r], dst_ref=chunks.at[slot],
            send_sem=z_send.at[peer], recv_sem=z_recv.at[slot],
            device_id=(peer, c), device_id_type=mesh_id)

    def z_start(n):
        along_z(lax.rem(r + n + 1, rows_n), r).start()
    each(rows_n - 1, z_start)

    def along_row(peer, source):
        return pltpu.make_async_remote_copy(
            src_ref=chunks.at[r], dst_ref=factor_ref.at[at(source), :],
            send_sem=row_send.at[peer], recv_sem=row_recv.at[source],
            device_id=(r, peer), device_id_type=mesh_id)

    def row_start(n):
        peer = lax.rem(c + n + 1, cols_n)

        @pl.when(peer != 0)
        def _():
            along_row(peer, c).start()
    each(cols_n - 1, row_start)
    mine = pltpu.make_async_copy(chunks.at[r], factor_ref.at[at(c), :], local_sem)

    @pl.when(c != 0)
    def _():
        mine.start()

    def match(k, slot):
        return pltpu.make_async_remote_copy(
            src_ref=chunks.at[k], dst_ref=across_ref.at[at(slot), :],
            send_sem=a_send.at[k], recv_sem=a_recv.at[slot],
            device_id=(r, ratio * k + c // per_width), device_id_type=mesh_id)

    def match_own(k):
        return pltpu.make_async_copy(
            chunks.at[k], across_ref.at[at(lax.rem(c, per_width)), :], a_local)

    def forward(n):
        k = lax.rem(r + n, rows_n)

        @pl.when(n != 0)
        def _():
            along_z(k, k).wait_recv()
        t = ratio * k + c // per_width

        @pl.when(t != c)
        def _():
            match(k, lax.rem(c, per_width)).start()

        @pl.when(t == c)
        def _():
            match_own(k).start()
    each(rows_n, forward)

    @pl.when(c != 0)
    def _():
        def from_row(n):
            peer = lax.rem(c + n + 1, cols_n)
            along_row(peer, peer).wait_recv()
        each(cols_n - 1, from_row)
        mine.wait()
        wait_tiles()

    @pl.when(c == 0)
    def _():
        whole.wait()
        each(cols_n - 1, lambda n: scatter(n + 1).wait_send())

    def from_match(i):
        source = lax.rem(c, ratio) * per_width + i

        @pl.when(source != c)
        def _():
            match(c // ratio, i).wait_recv()

        @pl.when(source == c)
        def _():
            match_own(c // ratio).wait()
    each(per_width, from_match)

    def sent_row(n):
        peer = lax.rem(c + n + 1, cols_n)

        @pl.when(peer != 0)
        def _():
            along_row(peer, c).wait_send()
    each(cols_n - 1, sent_row)

    def sent_z(n):
        along_z(lax.rem(r + n + 1, rows_n), r).wait_send()
    each(rows_n - 1, sent_z)

    def sent_match(k):
        @pl.when(ratio * k + c // per_width != c)
        def _():
            match(k, lax.rem(c, per_width)).wait_send()
    each(rows_n, sent_match)

    def sent_tiles(n):
        t = lax.rem(me + n + 1, total)
        tiles(t // cols_n, lax.rem(t, cols_n), me, t).wait_send()
    each(total - 1, sent_tiles)


def exchange(rtab, ctab, outgoing, diag, inverse, rows_n, cols_n, width):
    front_rows = diag.shape[0]
    height, panel = front_rows * BLK, inverse.shape[0]
    ratio = cols_n // rows_n
    smem = pl.BlockSpec(memory_space=pltpu.SMEM)
    vmem = pl.BlockSpec(memory_space=pltpu.VMEM)
    hbm = pl.BlockSpec(memory_space=pl.ANY)
    dma = pltpu.SemaphoreType.DMA
    return pl.pallas_call(
        functools.partial(exchange_kernel, rows_n=rows_n, cols_n=cols_n, front_rows=front_rows,
                          front_cols=width // BLK, panel_cols=panel // BLK),
        in_specs=[smem, smem, hbm, vmem, vmem],
        out_specs=[hbm, hbm, hbm],
        out_shape=[
            jax.ShapeDtypeStruct(outgoing.shape, jnp.float32),
            jax.ShapeDtypeStruct((height, panel), jnp.float32),
            jax.ShapeDtypeStruct((width, panel), jnp.float32),
        ],
        scratch_shapes=[
            pltpu.VMEM(outgoing.shape, jnp.float32),
            pltpu.VMEM((height, panel), jnp.float32),
            pltpu.VMEM((height, panel), jnp.float32),
            pltpu.VMEM((rows_n, height // cols_n, panel), jnp.float32),
            pltpu.VMEM((panel, panel), jnp.bfloat16),
            pltpu.VMEM((panel, panel), jnp.bfloat16),
            dma((rows_n * cols_n,)), dma((rows_n * cols_n,)), dma, dma,
            dma((cols_n,)), dma,
            dma((rows_n,)), dma((rows_n,)),
            dma((cols_n,)), dma((cols_n,)),
            dma((rows_n,)), dma((cols_n // ratio,)),
            dma, dma,
        ],
        compiler_params=pltpu.CompilerParams(
            collective_id=0, has_side_effects=True, vmem_limit_bytes=56 * MIB),
    )(rtab, ctab, outgoing, diag, inverse)


def tables(block_map, row_count, col_count, row_items, col_items, front_rows, front_cols,
           per_row, per_col, my_row, my_col):
    half = col_count // 2
    child_blocks = block_map.shape[1]
    cap = per_row * per_col
    child = jnp.where(my_col >= half, block_map[1], block_map[0])
    row_parent = pick(
        (my_col % half * row_items + jnp.arange(row_items))[:, None] == jnp.arange(child_blocks)[None, :],
        child[None, :],
    )
    col_parent = pick(
        (my_row * col_items + jnp.arange(col_items))[:, None] == jnp.arange(child_blocks)[None, :],
        child[None, :],
    )
    rowsel = selection(row_parent // front_rows, row_count, per_row)
    colsel = selection(col_parent // front_cols, col_count, per_col)
    ids = jnp.arange(child_blocks, dtype=jnp.int32)
    row_rank = ranks((block_map // front_rows).reshape(2, -1, row_items)).reshape(2, -1)
    col_rank = ranks((block_map // front_cols).reshape(2, -1, col_items)).reshape(2, -1)
    source_col = jnp.arange(2, dtype=jnp.int32)[:, None] * half + ids[None, :] // row_items
    row_value = source_col * cap + row_rank * per_col
    col_value = (ids[None, :] // col_items) * (col_count * cap) + col_rank
    at_row = block_map[:, None, :] == (my_row * front_rows + jnp.arange(front_rows))[None, :, None]
    at_col = block_map[:, None, :] == (my_col * front_cols + jnp.arange(front_cols))[None, :, None]
    rtab = pick(at_row, row_value[:, None, :] + 1) - 1
    ctab = pick(at_col, col_value[:, None, :] + 1) - 1
    return rowsel, colsel, rtab.reshape(-1), ctab.reshape(-1)


def on_device(updates, block_map, own_diag, panel_inverse):
    row_count, col_count = lax.axis_size("row"), lax.axis_size("col")
    my_row, my_col = lax.axis_index("row"), lax.axis_index("col")
    devices = row_count * col_count
    row_items, col_items = updates.shape[0] // BLK, updates.shape[1] // BLK
    per_row, per_col = max(1, row_items // row_count), max(1, col_items // col_count)
    height = own_diag.shape[0]
    width = height * row_count // col_count
    panel = panel_inverse.shape[0]
    front_rows, front_cols = height // BLK, width // BLK
    rowsel, colsel, rtab, ctab = tables(
        block_map, row_count, col_count, row_items, col_items, front_rows, front_cols,
        per_row, per_col, my_row, my_col,
    )
    dtab = jnp.stack([my_row * front_rows, my_col * front_cols]).astype(jnp.int32)
    diag = own_diag.reshape(front_rows, BLK)
    outgoing = pack(updates, rowsel, colsel, row_count, col_count, per_row, per_col)
    incoming, factor, across = exchange(
        rtab, ctab, outgoing.reshape(devices, per_row * per_col, BLK, BLK), diag, panel_inverse,
        row_count, col_count, width,
    )
    incoming = incoming.reshape(-1, BLK, BLK)
    return tuple(finish(rtab, ctab, dtab, incoming, diag, factor, across))


def solution(mesh):
    return jax.shard_map(
        on_device,
        mesh=mesh,
        in_specs=(P("col", "row"), P(), P("row"), P()),
        out_specs=(P("row", None), P("row", "col")),
        check_vma=False,
    )
```
